32 devices in a mesh: groups: 2 (over y), tiles: 4 (over z), rep: 4 (over x, core).
Axes of the slice: x: 2, y: 2, z: 4, core: 2. Of those that a mesh axis runs over, the one named last changes fastest.
Arguments:
- tiles: float32 [512, 256, 256], P(('groups', 'tiles', 'rep')), parts along dimension 0, may hold values from 0 to 1, as said below
- tile_row: int32 [512], P(('groups', 'tiles', 'rep')), parts along dimension 0, may hold values from 0 to 15, as said below
- tile_col: int32 [512], P(('groups', 'tiles', 'rep')), parts along dimension 0, may hold values from 0 to 15
- scaling: float32 [8192], P(('groups', 'tiles')), parts along dimension 0, may hold values from 0.3 to 3
Outputs:
- balanced: float32 [8192], P(('groups', 'tiles')), parts along dimension 0
- residual: float32 [8192], P(('groups', 'tiles')), parts along dimension 0
The draws below stay inside these ranges and needn't reach their ends.
There are 2 independent parts, one for each index of `groups`. The reference program is written for one: setup_inputs(seed, part) draws one part's arguments, and reference() takes and returns one part's arrays. A program takes and returns all parts, laid end to end along the dimension named above; each array names one. Nothing has to cross between parts.
Inputs may be any that keep to these rules, and one draw needn't show every extreme that they name: `tile_row`: blocks of index q of tiles are q * 4 to q * 4 + 3. A tile's row block is at most its column block. Outside the blocks of its own index of tiles and the two indices beside it, the tiles of one device name at most 26 blocks of each index, counted with repetition. `tiles`: entries are not negative.
All inputs are finite; a program needn't handle non-finite values.
Results may differ from the reference program's by a relative error of at most 0.0003.
Values sent between devices are 32-bit elements; how exact they have to be, the bound alone decides.
A program may use at most 64 MiB of HBM per device.

```python
import math
import jax
import jax.numpy as jnp
from jax import lax

TB = 256
BPD = 4
TPD = 16
REACH = 4
ITERS = 2
NB = 16
NT = 256
N = 4096


def tile_layout(key):
    devices = NT // TPD
    owners = NB // BPD
    far_tiles = TPD - 3
    spread = owners - 3
    device = jnp.arange(devices, dtype=jnp.int32)
    place = device // BPD
    lane = device % BPD
    first, second, third = jax.random.split(key, 3)
    centre = BPD * place + lane
    reach = jax.random.randint(first, (devices,), 2, REACH + 1).astype(jnp.int32)
    row_one = jnp.minimum(centre, NB - 2)
    col_one = row_one + 1
    row_two = jnp.where(centre >= reach, centre - reach, centre)
    col_two = jnp.where(centre >= reach, centre, centre + reach)
    order = jax.vmap(lambda sub: jax.random.permutation(sub, spread))(jax.random.split(second, devices)).astype(jnp.int32)
    chosen = order[:, jnp.arange(2 * far_tiles) % spread]
    peer = (place[:, None] + 2 + chosen) % owners
    ends = peer * BPD + jax.random.randint(third, (devices, 2 * far_tiles), 0, BPD).astype(jnp.int32)
    pairs = ends.reshape(devices, far_tiles, 2)
    row_far = jnp.minimum(pairs[:, :, 0], pairs[:, :, 1])
    col_far = jnp.maximum(pairs[:, :, 0], pairs[:, :, 1])
    rows = jnp.concatenate([centre[:, None], row_one[:, None], row_two[:, None], row_far], axis=1).reshape(-1)
    cols = jnp.concatenate([centre[:, None], col_one[:, None], col_two[:, None], col_far], axis=1).reshape(-1)
    return (rows.astype(jnp.int32), cols.astype(jnp.int32))


def draw_tile_row(key, part):
    rows, cols = tile_layout(key)
    return rows


def draw_tile_col(key, part):
    rows, cols = tile_layout(key)
    return cols


def draw_tiles(key, part):
    key = jax.random.fold_in(key, 7)
    shape = (NT, TB, TB)
    base = jnp.exp(jax.random.uniform(key, shape, jnp.float32, math.log(0.05), 0.0))
    slot = jnp.arange(NT) % TPD
    mirrored = 0.5 * (base + jnp.swapaxes(base, 1, 2))
    base = jnp.where((slot == 0)[:, None, None], mirrored, base)
    table = jnp.array([0.6, 0.45, 0.35], jnp.float32)
    factor = jnp.where(slot < 3, table[jnp.minimum(slot, 2)], 0.04) / TB
    return base * factor[:, None, None]


def level_of(rng, shape, cuts, least, high):
    def one(dim, parts):
        steps = jax.random.uniform(jax.random.fold_in(jax.random.fold_in(rng, 6), dim), (parts,), jnp.float32, least / len(cuts), high / len(cuts))
        return jnp.repeat(jnp.exp(steps), shape[dim] // parts).reshape((-1,) + (1,) * (len(shape) - dim - 1))

    factor_of = one(*cuts[0])
    for cut in cuts[1:]:
        factor_of = factor_of * one(*cut)
    return factor_of


def setup_inputs(seed: int = 0, part: int = 0) -> dict:
    seeds = jax.random.split(jax.random.key(seed), 5)
    own_keys = jax.random.split(jax.random.fold_in(seeds[4], part), 5)
    tiles = draw_tiles(jax.random.fold_in(jax.random.fold_in(seeds[4], part), 71), part)
    tile_row = draw_tile_row(jax.random.fold_in(jax.random.fold_in(seeds[4], part), 71), part)
    tile_col = draw_tile_col(jax.random.fold_in(jax.random.fold_in(seeds[4], part), 71), part)
    scaling = jnp.clip(jnp.exp(math.log(3.0) - 2.3025851 * jax.random.uniform(own_keys[3], (N,), jnp.float32) ** level_of(own_keys[3], (N,), ((0, 4),), -0.2, 0.2)), 0.3, 3.0)
    return {"tiles": tiles, "tile_row": tile_row, "tile_col": tile_col, "scaling": scaling}


def apply_map(tiles, tile_row, tile_col, vector):
    blocks = vector.reshape(NB, TB)
    forward = jnp.einsum('kij,kj->ki', tiles, blocks[tile_col], precision=lax.Precision.HIGHEST)
    backward = jnp.einsum('kij,ki->kj', tiles, blocks[tile_row], precision=lax.Precision.HIGHEST)
    backward = jnp.where((tile_row != tile_col)[:, None], backward, jnp.zeros_like(backward))
    total = jnp.zeros_like(blocks).at[tile_row].add(forward).at[tile_col].add(backward)
    return total.reshape(-1)


def reference(tiles, tile_row, tile_col, scaling):
    load = scaling * apply_map(tiles, tile_row, tile_col, scaling)
    residual = 1.0 - load
    direction = residual
    update = jnp.zeros_like(scaling)
    norm_now = jnp.sum(residual * residual)
    for step in range(ITERS):
        image = scaling * apply_map(tiles, tile_row, tile_col, scaling * direction) + load * direction
        alpha = norm_now / jnp.sum(direction * image)
        update = update + alpha * direction
        residual = residual - alpha * image
        norm_next = jnp.sum(residual * residual)
        direction = residual + (norm_next / norm_now) * direction
        norm_now = norm_next
    return scaling * (1.0 + update), residual
```

```python
import functools
import jax
import jax.numpy as jnp
from jax import lax
from jax.experimental import pallas as pl
from jax.experimental.pallas import tpu as pltpu
from jax.sharding import PartitionSpec as P

ITERS = 2
LANES = 128
MESH = pl.DeviceIdType.MESH


def split_exact(x):
    high = x.astype(jnp.bfloat16)
    rest = x - high.astype(jnp.float32)
    mid = rest.astype(jnp.bfloat16)
    low = (rest - mid.astype(jnp.float32)).astype(jnp.bfloat16)
    return jnp.concatenate([high, mid, low], axis=0)


def kernel(sizes, tiles_hbm, row_ref, col_ref, scaling_hbm, balanced_hbm, residual_hbm,
           mats, pick, spread, dense, shares, vectors, result,
           tile_sem, scale_sem, send_sem, recv_sem, out_sem):
    count, blocks, reps, owned, halves = sizes
    places = blocks // owned
    peers = places * reps
    q = lax.axis_index("tiles")
    r = lax.axis_index("rep")
    me = q * reps + r
    rows = blocks * halves
    width = halves * LANES

    def peer_id(offset):
        other = lax.rem(me + offset, peers)
        return other, {"tiles": other // reps, "rep": lax.rem(other, reps)}

    def tile_copy(k):
        return pltpu.make_async_copy(tiles_hbm.at[k], mats.at[count + k], tile_sem.at[k])

    for k in range(count):
        tile_copy(k).start()
    own = pl.ds(q * owned, owned)
    own_scale = pltpu.make_async_copy(scaling_hbm, vectors.at[0, own], scale_sem)
    own_scale.start()

    barrier = pltpu.get_barrier_semaphore()

    @pl.loop(1, peers)
    def _(offset):
        _, target = peer_id(offset)
        pl.semaphore_signal(barrier, inc=1, device_id=target, device_id_type=MESH)

    half_row = lax.broadcasted_iota(jnp.int32, (rows, width), 0)
    half = lax.broadcasted_iota(jnp.int32, (rows, width), 1) // LANES

    @pl.loop(0, count)
    def _(k):
        row, col = row_ref[k], col_ref[k]
        ahead = jnp.where(half_row == halves * col + half, 1.0, 0.0)
        wanted = jnp.where(row != col, halves * row, -halves)
        back = jnp.where(half_row == wanted + half, 1.0, 0.0)
        for part in range(3):
            pick[k, part * rows:(part + 1) * rows, :] = ahead.astype(jnp.bfloat16)
            pick[count + k, part * rows:(part + 1) * rows, :] = back.astype(jnp.bfloat16)

    pl.semaphore_wait(barrier, peers - 1)

    @pl.loop(1, places)
    def _(offset):
        pltpu.make_async_remote_copy(
            src_ref=scaling_hbm, dst_ref=vectors.at[0, own],
            send_sem=send_sem.at[0], recv_sem=recv_sem.at[0],
            device_id={"tiles": lax.rem(q + offset, places)}, device_id_type=MESH,
        ).start()

    @pl.loop(0, count)
    def _(k):
        tile_copy(k).wait()
        mats[k] = mats[count + k].T

    own_scale.wait()
    others = pl.ds(0, (places - 1) * owned)
    pltpu.make_async_copy(vectors.at[0, others], vectors.at[0, others], recv_sem.at[0]).wait()

    def read(slot):
        return vectors[slot].reshape(rows, LANES)

    line = lax.broadcasted_iota(jnp.int32, (rows, LANES), 0)
    rest = pl.ds(0, peers - 1)

    def apply_map(vector, turn):
        parts = split_exact(vector)

        def widen(k, carry):
            wide = lax.dot_general(parts, pick[k], (((0,), (0,)), ((), ())),
                                   preferred_element_type=jnp.float32)
            for h in range(halves):
                spread[k, h * LANES:(h + 1) * LANES, :] = wide[:, h * LANES:(h + 1) * LANES]
            return carry

        lax.fori_loop(0, 2 * count, widen, 0, unroll=8)

        def one(matrix, place, total):
            x = spread[matrix].reshape(-1, 8, LANES)
            for h in range(halves):
                block = mats[matrix, :, h * LANES:(h + 1) * LANES].reshape(-1, 8, LANES)
                product = jnp.sum(jnp.sum(block * x, axis=0), axis=0, keepdims=True)
                total = total + jnp.where(line == halves * place + h, product, 0.0)
            return total

        def both(k, total):
            total = one(k, row_ref[k], total)
            return one(count + k, col_ref[k], total)

        total = lax.fori_loop(0, count, both, jnp.zeros((rows, LANES), jnp.float32), unroll=2)
        dense[turn] = total.reshape(blocks, halves, LANES)
        shares[turn, me] = dense[turn, me]

        @pl.loop(1, peers)
        def _(offset):
            other, target = peer_id(offset)
            pltpu.make_async_remote_copy(
                src_ref=dense.at[turn, other], dst_ref=shares.at[turn, me],
                send_sem=send_sem.at[1 + 2 * turn], recv_sem=recv_sem.at[1 + 2 * turn],
                device_id=target, device_id_type=MESH,
            ).start()

        pltpu.make_async_copy(shares.at[turn, rest], shares.at[turn, rest], recv_sem.at[1 + 2 * turn]).wait()
        vectors[1 + turn, me] = jnp.sum(shares[turn], axis=0)

        @pl.loop(1, peers)
        def _(offset):
            _, target = peer_id(offset)
            pltpu.make_async_remote_copy(
                src_ref=vectors.at[1 + turn, me], dst_ref=vectors.at[1 + turn, me],
                send_sem=send_sem.at[2 + 2 * turn], recv_sem=recv_sem.at[2 + 2 * turn],
                device_id=target, device_id_type=MESH,
            ).start()

        pltpu.make_async_copy(vectors.at[1 + turn, rest], vectors.at[1 + turn, rest], recv_sem.at[2 + 2 * turn]).wait()
        return read(1 + turn)

    def inner(a, b):
        return jnp.sum(a * b, keepdims=True)

    scaling = read(0)
    load = scaling * apply_map(scaling, 0)
    residual = 1.0 - load
    direction = residual
    update = jnp.zeros_like(load)
    norm_now = inner(residual, residual)
    for step in range(ITERS):
        image = scaling * apply_map(scaling * direction, 1 + step) + load * direction
        alpha = norm_now / inner(direction, image)
        update = update + alpha * direction
        residual = residual - alpha * image
        if step + 1 < ITERS:
            norm_next = inner(residual, residual)
            direction = residual + (norm_next / norm_now) * direction
            norm_now = norm_next
    result[0] = (scaling * (1.0 + update)).reshape(blocks, halves, LANES)
    result[1] = residual.reshape(blocks, halves, LANES)
    outs = [pltpu.make_async_copy(result.at[i, own], ref, out_sem.at[i])
            for i, ref in enumerate((balanced_hbm, residual_hbm))]
    for out in outs:
        out.start()
    pltpu.make_async_copy(vectors.at[0, others], vectors.at[0, others], send_sem.at[0]).wait()
    for turn in range(1 + ITERS):
        for phase in range(2):
            pltpu.make_async_copy(shares.at[turn, rest], shares.at[turn, rest],
                                  send_sem.at[1 + 2 * turn + phase]).wait()
    for out in outs:
        out.wait()


def shards(places, reps, tiles, tile_row, tile_col, scaling):
    count, width, _ = tiles.shape
    halves = width // LANES
    owned = scaling.shape[0] // width
    blocks = owned * places
    assert owned == reps
    rows = blocks * halves
    turns = 1 + ITERS
    any_space = pl.BlockSpec(memory_space=pl.ANY)
    smem = pl.BlockSpec(memory_space=pltpu.SMEM)
    shape = jax.ShapeDtypeStruct((owned, halves, LANES), jnp.float32)
    balanced, residual = pl.pallas_call(
        functools.partial(kernel, (count, blocks, reps, owned, halves)),
        out_shape=(shape, shape),
        in_specs=[any_space, smem, smem, any_space],
        out_specs=(any_space, any_space),
        scratch_shapes=[
            pltpu.VMEM((2 * count, width, width), jnp.float32),
            pltpu.VMEM((2 * count, 3 * rows, width), jnp.bfloat16),
            pltpu.VMEM((2 * count, width, LANES), jnp.float32),
            pltpu.VMEM((turns, blocks, halves, LANES), jnp.float32),
            pltpu.VMEM((turns, blocks, halves, LANES), jnp.float32),
            pltpu.VMEM((1 + turns, blocks, halves, LANES), jnp.float32),
            pltpu.VMEM((2, blocks, halves, LANES), jnp.float32),
            pltpu.SemaphoreType.DMA((count,)),
            pltpu.SemaphoreType.DMA,
            pltpu.SemaphoreType.DMA((1 + 2 * turns,)),
            pltpu.SemaphoreType.DMA((1 + 2 * turns,)),
            pltpu.SemaphoreType.DMA((2,)),
        ],
        compiler_params=pltpu.CompilerParams(
            collective_id=0, has_side_effects=True, vmem_limit_bytes=52 * 2**20),
    )(tiles, tile_row, tile_col, scaling.reshape(owned, halves, LANES))
    return balanced.reshape(-1), residual.reshape(-1)


def solution(mesh):
    placed = (
        P(("groups", "tiles", "rep"), None, None),
        P(("groups", "tiles", "rep")),
        P(("groups", "tiles", "rep")),
        P(("groups", "tiles")),
    )
    return jax.shard_map(
        functools.partial(shards, mesh.shape["tiles"], mesh.shape["rep"]),
        mesh=mesh,
        in_specs=placed,
        out_specs=(P(("groups", "tiles")), P(("groups", "tiles"))),
        check_vma=False,
    )
```

```python
import functools
import jax
import jax.numpy as jnp
from jax import lax
from jax.experimental import pallas as pl
from jax.experimental.pallas import tpu as pltpu
from jax.sharding import PartitionSpec as P

ITERS = 2
LANES = 128
MESH = pl.DeviceIdType.MESH


def split_exact(x):
    high = x.astype(jnp.bfloat16)
    rest = x - high.astype(jnp.float32)
    mid = rest.astype(jnp.bfloat16)
    low = (rest - mid.astype(jnp.float32)).astype(jnp.bfloat16)
    return jnp.concatenate([high, mid, low], axis=0)


def wrap(index, size):
    return jnp.where(index >= size, index - size, index)


def kernel(sizes, tiles_hbm, row_ref, col_ref, scaling_ref, balanced_ref, residual_ref,
           mats, pick, spread, dense, mate, shares, vectors, state, ends, dots,
           tile_sem, scale_sem, send_sem, recv_sem, mate_send, mate_recv, dot_send, dot_recv):
    count, blocks, reps, owned, halves, paired = sizes
    places = blocks // owned
    q = lax.axis_index("tiles")
    r = lax.axis_index("rep")
    rows = blocks * halves
    width = halves * LANES
    chunk = pick.shape[0]
    lanes = 2 if paired else 1
    turn_reps = reps // lanes
    mine = r // lanes
    side = r - mine * lanes
    me = q * turn_reps + mine
    members = places * turn_reps
    final = ITERS if paired else -1

    def for_peers(act):
        def column(ahead, first):
            place = wrap(q + ahead, places)
            for turn in range(first, turn_reps):
                member = wrap(mine + turn, turn_reps)
                act(place, place * turn_reps + member, {"tiles": place, "rep": member * lanes + side})

        if places <= 8:
            for ahead in range(places - 1, 0, -1):
                column(ahead, 0)
        else:
            pl.loop(1, places)(lambda ahead: column(ahead, 0))
        column(0, 1)

    partner = {"rep": r + 1 - 2 * side}

    def tile_copy(k):
        return pltpu.make_async_copy(tiles_hbm.at[k], mats.at[count + k], tile_sem.at[k])

    barrier = pltpu.get_barrier_semaphore()

    @for_peers
    def _(place, member, target):
        pl.semaphore_signal(barrier, inc=1, device_id=target, device_id_type=MESH)

    if paired:
        pl.semaphore_signal(barrier, inc=1, device_id=partner, device_id_type=MESH)

    for k in range(count):
        tile_copy(k).start()
    own = pl.ds(q * owned, owned)
    own_scale = pltpu.make_async_copy(scaling_ref, vectors.at[0, own], scale_sem)
    own_scale.start()

    half_row = lax.broadcasted_iota(jnp.int32, (chunk * halves, width), 0)
    half = lax.broadcasted_iota(jnp.int32, (chunk * halves, width), 1) // LANES

    @pl.loop(0, chunk)
    def _(b):
        hot = jnp.where(half_row == halves * b + half, 1.0, 0.0).astype(jnp.bfloat16)
        pick[b] = jnp.concatenate([hot, hot, hot], axis=0)

    pl.semaphore_wait(barrier, members if paired else members - 1)

    for ahead in range(places - 1, 0, -1):
        pltpu.make_async_remote_copy(
            src_ref=scaling_ref, dst_ref=vectors.at[0, own],
            send_sem=send_sem.at[0], recv_sem=recv_sem.at[0],
            device_id={"tiles": wrap(q + ahead, places)}, device_id_type=MESH,
        ).start()

    @pl.loop(0, count)
    def _(k):
        tile_copy(k).wait()
        mats[k] = mats[count + k].T

    own_scale.wait()
    others = pl.ds(0, (places - 1) * owned)
    rest = pl.ds(0, members - 1)
    pltpu.make_async_copy(vectors.at[0, others], vectors.at[0, others], recv_sem.at[0]).wait()

    line = lax.broadcasted_iota(jnp.int32, (rows, LANES), 0)

    def products(vector):
        for first in range(0, blocks, chunk):
            parts = split_exact(vector[first * halves:(first + chunk) * halves]).T

            def widen(b, carry):
                wide = jnp.dot(parts, pick[b], preferred_element_type=jnp.float32)
                for h in range(halves):
                    spread[first + b, h * LANES:(h + 1) * LANES, :] = wide[:, h * LANES:(h + 1) * LANES]
                return carry

            lax.fori_loop(0, chunk, widen, 0, unroll=True)

        def one(matrix, source, place, total):
            x = spread[source].reshape(-1, 8, LANES)
            for h in range(halves):
                block = mats[matrix, :, h * LANES:(h + 1) * LANES].reshape(-1, 8, LANES)
                product = jnp.sum(jnp.sum(block * x, axis=0), axis=0, keepdims=True)
                total = total + jnp.where(line == halves * place + h, product, 0.0)
            return total

        def both(k, total):
            row, col = row_ref[k], col_ref[k]
            total = one(k, col, row, total)
            return one(count + k, row, jnp.where(row == col, -1, col), total)

        return lax.fori_loop(0, count, both, jnp.zeros((rows, LANES), jnp.float32), unroll=2)

    def with_partner(total, turn):
        dense[turn] = total.reshape(blocks, halves, LANES)
        swap = pltpu.make_async_remote_copy(
            src_ref=dense.at[turn], dst_ref=mate.at[turn],
            send_sem=mate_send.at[turn], recv_sem=mate_recv.at[turn],
            device_id=partner, device_id_type=MESH)
        swap.start()
        swap.wait()
        return total + mate[turn].reshape(rows, LANES)

    def send(source, target_ref, slot, device):
        pltpu.make_async_remote_copy(
            src_ref=source, dst_ref=target_ref, send_sem=send_sem.at[slot],
            recv_sem=recv_sem.at[slot], device_id=device, device_id_type=MESH,
        ).start()

    def take(ref, semaphore):
        pltpu.make_async_copy(ref, ref, semaphore).wait()

    def summed_pairs(vector, turn):
        total = with_partner(products(vector), turn)
        shares[turn, me] = total.reshape(blocks, halves, LANES)

        @for_peers
        def _(place, member, target):
            send(shares.at[turn, me], shares.at[turn, me], 1 + turn, target)

        take(shares.at[turn, rest], recv_sem.at[1 + turn])
        return jnp.sum(shares[turn], axis=0).reshape(rows, LANES)

    def summed_blocks(vector, turn):
        dense[turn] = products(vector).reshape(blocks, halves, LANES)
        shares[turn, me] = dense[turn, me]
        slot = 1 + 2 * turn

        @for_peers
        def _(place, member, target):
            send(dense.at[turn, member], shares.at[turn, me], slot, target)

        take(shares.at[turn, rest], recv_sem.at[slot])
        vectors[1 + turn, me] = jnp.sum(shares[turn], axis=0)

        @for_peers
        def _(place, member, target):
            send(vectors.at[1 + turn, me], vectors.at[1 + turn, me], slot + 1, target)

        take(vectors.at[1 + turn, rest], recv_sem.at[slot + 1])
        return vectors[1 + turn].reshape(rows, LANES)

    apply_map = summed_pairs if paired else summed_blocks

    def inner(a, b):
        return jnp.sum(a * b, keepdims=True)

    scaling = vectors[0].reshape(rows, LANES)
    load = scaling * apply_map(scaling, 0)
    residual = 1.0 - load
    direction = residual
    update = jnp.zeros_like(load)
    norm_now = inner(residual, residual)
    for step in range(ITERS):
        turn = 1 + step
        if turn == final:
            break
        image = scaling * apply_map(scaling * direction, turn) + load * direction
        alpha = norm_now / inner(direction, image)
        update = update + alpha * direction
        residual = residual - alpha * image
        if step + 1 < ITERS:
            norm_next = inner(residual, residual)
            direction = residual + (norm_next / norm_now) * direction
            norm_now = norm_next

    kept = [scaling * (1.0 + update), residual]
    if paired:
        kept += [scaling, load * direction, direction]
    for i, value in enumerate(kept):
        state[i] = value.reshape(blocks, halves, LANES)
    if paired:
        scaled = scaling * direction
        known = inner(load * direction, direction)
        total = with_partner(products(scaled), final)
        dense[1 + final] = total.reshape(blocks, halves, LANES)
        ends[me] = dense[1 + final, own]
        dots[me] = jnp.broadcast_to(inner(scaled, total), (1, LANES))

        @for_peers
        def _(place, member, target):
            send(dense.at[1 + final, pl.ds(place * owned, owned)], ends.at[me], 1 + final, target)
            pltpu.make_async_remote_copy(
                src_ref=dots.at[me], dst_ref=dots.at[me], send_sem=dot_send,
                recv_sem=dot_recv, device_id=target, device_id_type=MESH,
            ).start()

        take(dots.at[rest], dot_recv)
        alpha = norm_now / (known + jnp.sum(dots[...], axis=0)[:, :1])
        take(ends.at[rest], recv_sem.at[1 + final])
        image = state[2, own] * jnp.sum(ends[...], axis=0) + state[3, own]
        balanced_ref[...] = state[0, own] + state[2, own] * (alpha * state[4, own])
        residual_ref[...] = state[1, own] - alpha * image
    else:
        balanced_ref[...] = state[0, own]
        residual_ref[...] = state[1, own]

    take(vectors.at[0, others], send_sem.at[0])
    if paired:
        for turn in range(final):
            take(shares.at[turn, rest], send_sem.at[1 + turn])
        take(ends.at[rest], send_sem.at[1 + final])
        take(dots.at[rest], dot_send)
    else:
        for slot in range(1, 3 + 2 * ITERS):
            take(shares.at[0, rest], send_sem.at[slot])


def shards(places, reps, tiles, tile_row, tile_col, scaling):
    count, width, _ = tiles.shape
    halves = width // LANES
    owned = scaling.shape[0] // width
    blocks = owned * places
    assert owned == reps
    turns = 1 + ITERS
    paired = reps % 2 == 0 and places * reps <= 32
    chunk = 16 if blocks % 16 == 0 else blocks
    members = blocks // 2 if paired else blocks
    block = (halves, LANES)
    any_space = pl.BlockSpec(memory_space=pl.ANY)
    smem = pl.BlockSpec(memory_space=pltpu.SMEM)
    vmem = pl.BlockSpec(memory_space=pltpu.VMEM)
    shape = jax.ShapeDtypeStruct((owned,) + block, jnp.float32)
    slots = 1 + 2 * turns

    def scratch(*dims):
        return pltpu.VMEM(dims + block, jnp.float32)

    balanced, residual = pl.pallas_call(
        functools.partial(kernel, (count, blocks, reps, owned, halves, paired)),
        out_shape=(shape, shape),
        in_specs=[any_space, smem, smem, any_space],
        out_specs=(vmem, vmem),
        scratch_shapes=[
            pltpu.VMEM((2 * count, width, width), jnp.float32),
            pltpu.VMEM((chunk, 3 * chunk * halves, width), jnp.bfloat16),
            pltpu.VMEM((blocks, width, LANES), jnp.float32),
            scratch(turns + 1, blocks),
            scratch(turns, blocks),
            scratch(turns, members, blocks) if paired else scratch(turns, members),
            scratch(1 + turns, blocks),
            scratch(5, blocks),
            scratch(members, owned),
            pltpu.VMEM((members, 1, LANES), jnp.float32),
            pltpu.SemaphoreType.DMA((count,)),
            pltpu.SemaphoreType.DMA,
            pltpu.SemaphoreType.DMA((slots,)),
            pltpu.SemaphoreType.DMA((slots,)),
            pltpu.SemaphoreType.DMA((turns,)),
            pltpu.SemaphoreType.DMA((turns,)),
            pltpu.SemaphoreType.DMA,
            pltpu.SemaphoreType.DMA,
        ],
        compiler_params=pltpu.CompilerParams(
            collective_id=0, has_side_effects=True, vmem_limit_bytes=56 * 2**20),
    )(tiles, tile_row, tile_col, scaling.reshape((owned,) + block))
    return balanced.reshape(-1), residual.reshape(-1)


def solution(mesh):
    placed = (
        P(("groups", "tiles", "rep"), None, None),
        P(("groups", "tiles", "rep")),
        P(("groups", "tiles", "rep")),
        P(("groups", "tiles")),
    )
    return jax.shard_map(
        functools.partial(shards, mesh.shape["tiles"], mesh.shape["rep"]),
        mesh=mesh,
        in_specs=placed,
        out_specs=(P(("groups", "tiles")), P(("groups", "tiles"))),
        check_vma=False,
    )
```

```python
import functools
import jax
import jax.numpy as jnp
from jax import lax
from jax.experimental import pallas as pl
from jax.experimental.pallas import tpu as pltpu
from jax.sharding import PartitionSpec as P

ITERS = 2
LANES = 128
MESH = pl.DeviceIdType.MESH


def split_exact(x):
    high = x.astype(jnp.bfloat16)
    rest = x - high.astype(jnp.float32)
    mid = rest.astype(jnp.bfloat16)
    low = (rest - mid.astype(jnp.float32)).astype(jnp.bfloat16)
    return jnp.concatenate([high, mid, low], axis=0)


def wrap(index, size):
    return jnp.where(index >= size, index - size, index)


def kernel(sizes, tiles_hbm, row_hbm, col_hbm, scaling_ref, out_ref,
           row_ref, col_ref,
           mats, pick, spread, dense, mate, shares, vectors, state, ends, dots,
           tile_sem, scale_sem, index_sem, send_sem, recv_sem, mate_send, mate_recv, dot_send, dot_recv):
    count, blocks, reps, owned, halves, paired = sizes
    places = blocks // owned
    q = lax.axis_index("tiles")
    r = lax.axis_index("rep")
    rows = blocks * halves
    width = halves * LANES
    chunk = pick.shape[0]
    lanes = 2 if paired else 1
    turn_reps = reps // lanes
    mine = r // lanes
    side = r - mine * lanes
    me = q * turn_reps + mine
    members = places * turn_reps
    final = ITERS if paired else -1

    def for_peers(act):
        def column(ahead, first):
            place = wrap(q + ahead, places)
            for turn in range(first, turn_reps):
                member = wrap(mine + turn, turn_reps)
                act(place, place * turn_reps + member, {"tiles": place, "rep": member * lanes + side})

        if places <= 8:
            for ahead in range(places - 1, 0, -1):
                column(ahead, 0)
        else:
            pl.loop(1, places)(lambda ahead: column(ahead, 0))
        column(0, 1)

    partner = {"rep": r + 1 - 2 * side}

    def tile_copy(k):
        return pltpu.make_async_copy(tiles_hbm.at[k], mats.at[count + k], tile_sem.at[k])

    barrier = pltpu.get_barrier_semaphore()

    @for_peers
    def _(place, member, target):
        pl.semaphore_signal(barrier, inc=1, device_id=target, device_id_type=MESH)

    if paired:
        pl.semaphore_signal(barrier, inc=1, device_id=partner, device_id_type=MESH)

    indices = [pltpu.make_async_copy(source, held, index_sem.at[i])
               for i, (source, held) in enumerate(((row_hbm, row_ref), (col_hbm, col_ref)))]
    for copy in indices:
        copy.start()
    for k in range(count):
        tile_copy(k).start()
    own = pl.ds(q * owned, owned)
    own_scale = pltpu.make_async_copy(scaling_ref, vectors.at[0, own], scale_sem)
    own_scale.start()

    half_row = lax.broadcasted_iota(jnp.int32, (chunk * halves, width), 0)
    half = lax.broadcasted_iota(jnp.int32, (chunk * halves, width), 1) // LANES

    @pl.loop(0, chunk)
    def _(b):
        hot = jnp.where(half_row == halves * b + half, 1.0, 0.0).astype(jnp.bfloat16)
        pick[b] = jnp.concatenate([hot, hot, hot], axis=0)

    own_scale.wait()
    for copy in indices:
        copy.wait()
    pl.semaphore_wait(barrier, members if paired else members - 1)

    for ahead in range(places - 1, 0, -1):
        pltpu.make_async_remote_copy(
            src_ref=vectors.at[0, own], dst_ref=vectors.at[0, own],
            send_sem=send_sem.at[0], recv_sem=recv_sem.at[0],
            device_id={"tiles": wrap(q + ahead, places)}, device_id_type=MESH,
        ).start()

    @pl.loop(0, count)
    def _(k):
        tile_copy(k).wait()
        mats[k] = mats[count + k].T

    others = pl.ds(0, (places - 1) * owned)
    rest = pl.ds(0, members - 1)
    pltpu.make_async_copy(vectors.at[0, others], vectors.at[0, others], recv_sem.at[0]).wait()

    line = lax.broadcasted_iota(jnp.int32, (rows, LANES), 0)

    def products(vector):
        for first in range(0, blocks, chunk):
            parts = split_exact(vector[first * halves:(first + chunk) * halves]).T

            def widen(b, carry):
                wide = jnp.dot(parts, pick[b], preferred_element_type=jnp.float32)
                for h in range(halves):
                    spread[first + b, h * LANES:(h + 1) * LANES, :] = wide[:, h * LANES:(h + 1) * LANES]
                return carry

            lax.fori_loop(0, chunk, widen, 0, unroll=True)

        def one(matrix, source, place, total):
            x = spread[source].reshape(-1, 8, LANES)
            for h in range(halves):
                block = mats[matrix, :, h * LANES:(h + 1) * LANES].reshape(-1, 8, LANES)
                product = jnp.sum(jnp.sum(block * x, axis=0), axis=0, keepdims=True)
                total = total + jnp.where(line == halves * place + h, product, 0.0)
            return total

        def both(k, total):
            row, col = row_ref[k], col_ref[k]
            total = one(k, col, row, total)
            return one(count + k, row, jnp.where(row == col, -1, col), total)

        return lax.fori_loop(0, count, both, jnp.zeros((rows, LANES), jnp.float32), unroll=8)

    def with_partner(total, turn):
        dense[turn] = total.reshape(blocks, halves, LANES)
        swap = pltpu.make_async_remote_copy(
            src_ref=dense.at[turn], dst_ref=mate.at[turn],
            send_sem=mate_send.at[turn], recv_sem=mate_recv.at[turn],
            device_id=partner, device_id_type=MESH)
        swap.start()
        swap.wait()
        return total + mate[turn].reshape(rows, LANES)

    def send(source, target_ref, slot, device):
        pltpu.make_async_remote_copy(
            src_ref=source, dst_ref=target_ref, send_sem=send_sem.at[slot],
            recv_sem=recv_sem.at[slot], device_id=device, device_id_type=MESH,
        ).start()

    def take(ref, semaphore):
        pltpu.make_async_copy(ref, ref, semaphore).wait()

    def summed_pairs(vector, turn):
        total = with_partner(products(vector), turn)
        shares[turn, me] = total.reshape(blocks, halves, LANES)

        @for_peers
        def _(place, member, target):
            send(shares.at[turn, me], shares.at[turn, me], 1 + turn, target)

        take(shares.at[turn, rest], recv_sem.at[1 + turn])
        return jnp.sum(shares[turn], axis=0).reshape(rows, LANES)

    def summed_blocks(vector, turn):
        dense[turn] = products(vector).reshape(blocks, halves, LANES)
        shares[turn, me] = dense[turn, me]
        slot = 1 + 2 * turn

        @for_peers
        def _(place, member, target):
            send(dense.at[turn, member], shares.at[turn, me], slot, target)

        take(shares.at[turn, rest], recv_sem.at[slot])
        vectors[1 + turn, me] = jnp.sum(shares[turn], axis=0)

        @for_peers
        def _(place, member, target):
            send(vectors.at[1 + turn, me], vectors.at[1 + turn, me], slot + 1, target)

        take(vectors.at[1 + turn, rest], recv_sem.at[slot + 1])
        return vectors[1 + turn].reshape(rows, LANES)

    apply_map = summed_pairs if paired else summed_blocks

    def inner(a, b):
        return jnp.sum(a * b, keepdims=True)

    scaling = vectors[0].reshape(rows, LANES)
    load = scaling * apply_map(scaling, 0)
    residual = 1.0 - load
    direction = residual
    update = jnp.zeros_like(load)
    norm_now = inner(residual, residual)
    for step in range(ITERS):
        turn = 1 + step
        if turn == final:
            break
        image = scaling * apply_map(scaling * direction, turn) + load * direction
        alpha = norm_now / inner(direction, image)
        update = update + alpha * direction
        residual = residual - alpha * image
        if step + 1 < ITERS:
            norm_next = inner(residual, residual)
            direction = residual + (norm_next / norm_now) * direction
            norm_now = norm_next

    kept = [scaling * (1.0 + update), residual]
    if paired:
        kept += [scaling, load * direction, direction]
    for i, value in enumerate(kept):
        state[i] = value.reshape(blocks, halves, LANES)
    if paired:
        scaled = scaling * direction
        known = inner(load * direction, direction)
        total = with_partner(products(scaled), final)
        dense[1 + final] = total.reshape(blocks, halves, LANES)
        ends[me] = dense[1 + final, own]
        dots[me] = jnp.broadcast_to(inner(scaled, total), (1, LANES))

        @for_peers
        def _(place, member, target):
            send(dense.at[1 + final, pl.ds(place * owned, owned)], ends.at[me], 1 + final, target)
            pltpu.make_async_remote_copy(
                src_ref=dots.at[me], dst_ref=dots.at[me], send_sem=dot_send,
                recv_sem=dot_recv, device_id=target, device_id_type=MESH,
            ).start()

        take(dots.at[rest], dot_recv)
        alpha = norm_now / (known + jnp.sum(dots[...], axis=0)[:, :1])
        take(ends.at[rest], recv_sem.at[1 + final])
        image = state[2, own] * jnp.sum(ends[...], axis=0) + state[3, own]
        out_ref[0] = state[0, own] + state[2, own] * (alpha * state[4, own])
        out_ref[1] = state[1, own] - alpha * image
    else:
        out_ref[0] = state[0, own]
        out_ref[1] = state[1, own]

    take(vectors.at[0, others], send_sem.at[0])
    if paired:
        for turn in range(final):
            take(shares.at[turn, rest], send_sem.at[1 + turn])
        take(ends.at[rest], send_sem.at[1 + final])
        take(dots.at[rest], dot_send)
    else:
        for slot in range(1, 3 + 2 * ITERS):
            take(shares.at[0, rest], send_sem.at[slot])


def shards(places, reps, tiles, tile_row, tile_col, scaling):
    count, width, _ = tiles.shape
    halves = width // LANES
    owned = scaling.shape[0] // width
    blocks = owned * places
    assert owned == reps
    turns = 1 + ITERS
    paired = reps % 2 == 0 and places * reps <= 32
    chunk = 16 if blocks % 16 == 0 else blocks
    members = blocks // 2 if paired else blocks
    block = (halves, LANES)
    hbm = pl.BlockSpec(memory_space=pltpu.HBM)
    vmem = pl.BlockSpec(memory_space=pltpu.VMEM)
    shape = jax.ShapeDtypeStruct((2, owned) + block, jnp.float32)
    slots = 1 + 2 * turns

    def scratch(*dims):
        return pltpu.VMEM(dims + block, jnp.float32)

    both = pl.pallas_call(
        functools.partial(kernel, (count, blocks, reps, owned, halves, paired)),
        out_shape=shape,
        in_specs=[hbm] * 4,
        out_specs=vmem,
        scratch_shapes=[
            pltpu.SMEM((count,), jnp.int32),
            pltpu.SMEM((count,), jnp.int32),
            pltpu.VMEM((2 * count, width, width), jnp.float32),
            pltpu.VMEM((chunk, 3 * chunk * halves, width), jnp.bfloat16),
            pltpu.VMEM((blocks, width, LANES), jnp.float32),
            scratch(turns + 1, blocks),
            scratch(turns, blocks),
            scratch(turns, members, blocks) if paired else scratch(turns, members),
            scratch(1 + turns, blocks),
            scratch(5, blocks),
            scratch(members, owned),
            pltpu.VMEM((members, 1, LANES), jnp.float32),
            pltpu.SemaphoreType.DMA((count,)),
            pltpu.SemaphoreType.DMA,
            pltpu.SemaphoreType.DMA((2,)),
            pltpu.SemaphoreType.DMA((slots,)),
            pltpu.SemaphoreType.DMA((slots,)),
            pltpu.SemaphoreType.DMA((turns,)),
            pltpu.SemaphoreType.DMA((turns,)),
            pltpu.SemaphoreType.DMA,
            pltpu.SemaphoreType.DMA,
        ],
        compiler_params=pltpu.CompilerParams(
            collective_id=0, has_side_effects=True, vmem_limit_bytes=56 * 2**20),
    )(tiles, tile_row, tile_col, scaling.reshape((owned,) + block))
    both = both.reshape(2, -1)
    return both[0], both[1]


def solution(mesh):
    placed = (
        P(("groups", "tiles", "rep"), None, None),
        P(("groups", "tiles", "rep")),
        P(("groups", "tiles", "rep")),
        P(("groups", "tiles")),
    )
    return jax.shard_map(
        functools.partial(shards, mesh.shape["tiles"], mesh.shape["rep"]),
        mesh=mesh,
        in_specs=placed,
        out_specs=(P(("groups", "tiles")), P(("groups", "tiles"))),
        check_vma=False,
    )
```

```python
import functools
import jax
import jax.numpy as jnp
from jax import lax
from jax.experimental import pallas as pl
from jax.experimental.pallas import tpu as pltpu
from jax.sharding import PartitionSpec as P

ITERS = 2
LANES = 128
MESH = pl.DeviceIdType.MESH


def split_exact(x):
    high = x.astype(jnp.bfloat16)
    rest = x - high.astype(jnp.float32)
    mid = rest.astype(jnp.bfloat16)
    low = (rest - mid.astype(jnp.float32)).astype(jnp.bfloat16)
    return jnp.concatenate([high, mid, low], axis=0)


def wrap(index, size):
    return jnp.where(index >= size, index - size, index)


def kernel(sizes, tiles_hbm, row_hbm, col_hbm, scaling_ref, out_ref,
           row_ref, col_ref,
           mats, pick, spread, scale_all, dense, mate, shares, state, ends, dots, terms, parcels, blocked,
           tile_sem, scale_sem, index_sem, send_sem, recv_sem, mate_send, mate_recv, dot_send, dot_recv):
    count, blocks, reps, owned, halves, paired = sizes
    places = blocks // owned
    q = lax.axis_index("tiles")
    r = lax.axis_index("rep")
    rows = blocks * halves
    width = halves * LANES
    chunk = pick.shape[0]
    lanes = 2 if paired else 1
    turn_reps = reps // lanes
    mine = r // lanes
    side = r - mine * lanes
    me = q * turn_reps + mine
    members = places * turn_reps
    final = ITERS if paired else -1

    def for_peers(act):
        def column(ahead, first):
            place = wrap(q + ahead, places)
            for turn in range(first, turn_reps):
                member = wrap(mine + turn, turn_reps)
                act(place, place * turn_reps + member, {"tiles": place, "rep": member * lanes + side})

        if places <= 8:
            for ahead in range(places - 1, 0, -1):
                column(ahead, 0)
        else:
            pl.loop(1, places)(lambda ahead: column(ahead, 0))
        column(0, 1)

    partner = {"rep": r + 1 - 2 * side}

    def send(source, target_ref, slot, device):
        pltpu.make_async_remote_copy(
            src_ref=source, dst_ref=target_ref, send_sem=send_sem.at[slot],
            recv_sem=recv_sem.at[slot], device_id=device, device_id_type=MESH,
        ).start()

    def take(ref, semaphore):
        pltpu.make_async_copy(ref, ref, semaphore).wait()

    def tile_copy(k):
        return pltpu.make_async_copy(tiles_hbm.at[k], mats.at[count + k], tile_sem.at[k])

    barrier = pltpu.get_barrier_semaphore()

    @for_peers
    def _(place, member, target):
        pl.semaphore_signal(barrier, inc=1, device_id=target, device_id_type=MESH)

    if paired:
        pl.semaphore_signal(barrier, inc=1, device_id=partner, device_id_type=MESH)

    indices = [pltpu.make_async_copy(source, held, index_sem.at[i])
               for i, (source, held) in enumerate(((row_hbm, row_ref), (col_hbm, col_ref)))]
    for copy in indices:
        copy.start()
    for k in range(count):
        tile_copy(k).start()
    held = owned * halves
    own = pl.ds(pl.multiple_of(q * held, held), held)
    own_scale = pltpu.make_async_copy(scaling_ref, scale_all.at[own], scale_sem)
    own_scale.start()

    half_row = lax.broadcasted_iota(jnp.int32, (chunk * halves, width), 0)
    half = lax.broadcasted_iota(jnp.int32, (chunk * halves, width), 1) // LANES

    @pl.loop(0, chunk)
    def _(b):
        hot = jnp.where(half_row == halves * b + half, 1.0, 0.0).astype(jnp.bfloat16)
        pick[b] = jnp.concatenate([hot, hot, hot], axis=0)

    own_scale.wait()
    for copy in indices:
        copy.wait()
    pl.semaphore_wait(barrier, members if paired else members - 1)

    for ahead in range(places - 1, 0, -1):
        pltpu.make_async_remote_copy(
            src_ref=scale_all.at[own], dst_ref=scale_all.at[own],
            send_sem=send_sem.at[0], recv_sem=recv_sem.at[0],
            device_id={"tiles": wrap(q + ahead, places)}, device_id_type=MESH,
        ).start()

    @pl.loop(0, count)
    def _(k):
        tile_copy(k).wait()
        mats[k] = mats[count + k].T

    others = scale_all.at[pl.ds(0, (places - 1) * held)]
    rest = pl.ds(0, members - 1)
    take(others, recv_sem.at[0])

    line = lax.broadcasted_iota(jnp.int32, (rows, LANES), 0)

    def products(vector):
        for first in range(0, blocks, chunk):
            parts = split_exact(vector[first * halves:(first + chunk) * halves]).T

            def widen(b, carry):
                wide = jnp.dot(parts, pick[b], preferred_element_type=jnp.float32)
                for h in range(halves):
                    spread[first + b, h * LANES:(h + 1) * LANES, :] = wide[:, h * LANES:(h + 1) * LANES]
                return carry

            lax.fori_loop(0, chunk, widen, 0, unroll=True)

        def one(matrix, source, place, total):
            x = spread[source].reshape(-1, 8, LANES)
            for h in range(halves):
                block = mats[matrix, :, h * LANES:(h + 1) * LANES].reshape(-1, 8, LANES)
                product = jnp.sum(jnp.sum(block * x, axis=0), axis=0, keepdims=True)
                total = total + jnp.where(line == halves * place + h, product, 0.0)
            return total

        def both(k, total):
            row, col = row_ref[k], col_ref[k]
            total = one(k, col, row, total)
            return one(count + k, row, jnp.where(row == col, -1, col), total)

        return lax.fori_loop(0, count, both, jnp.zeros((rows, LANES), jnp.float32), unroll=8)

    def with_partner(total, turn):
        dense[turn] = total
        pltpu.make_async_remote_copy(
            src_ref=dense.at[turn], dst_ref=mate.at[turn],
            send_sem=mate_send.at[turn], recv_sem=mate_recv.at[turn],
            device_id=partner, device_id_type=MESH).start()
        take(mate.at[turn], mate_recv.at[turn])
        return total + mate[turn]

    def summed_pairs(vector, turn):
        shares[turn, me] = with_partner(products(vector), turn)

        @for_peers
        def _(place, member, target):
            send(shares.at[turn, me], shares.at[turn, me], 1 + turn, target)

        take(shares.at[turn, rest], recv_sem.at[1 + turn])
        return jnp.sum(shares[turn], axis=0)

    def summed_blocks(vector, turn):
        terms[turn] = products(vector).reshape(blocks, halves, LANES)
        parcels[turn, me] = terms[turn, me]
        slot = 1 + 2 * turn

        @for_peers
        def _(place, member, target):
            send(terms.at[turn, member], parcels.at[turn, me], slot, target)

        take(parcels.at[turn, rest], recv_sem.at[slot])
        blocked[turn, me] = jnp.sum(parcels[turn], axis=0)

        @for_peers
        def _(place, member, target):
            send(blocked.at[turn, me], blocked.at[turn, me], slot + 1, target)

        take(blocked.at[turn, rest], recv_sem.at[slot + 1])
        return blocked[turn].reshape(rows, LANES)

    apply_map = summed_pairs if paired else summed_blocks

    def inner(a, b):
        return jnp.sum(a * b, keepdims=True)

    scaling = scale_all[...]
    load = scaling * apply_map(scaling, 0)
    residual = 1.0 - load
    direction = residual
    update = jnp.zeros_like(load)
    norm_now = inner(residual, residual)
    along = apply_map(scaling * direction, 1)
    across = along
    for step in range(ITERS):
        turn = 2 + step
        last = step + 1 == ITERS
        image = scaling * along + load * direction
        alpha = norm_now / inner(direction, image)
        update = update + alpha * direction
        residual = residual - alpha * image
        if last:
            break
        norm_next = inner(residual, residual)
        ratio = norm_next / norm_now
        direction = residual + ratio * direction
        norm_now = norm_next
        if turn == final:
            break
        across = across - alpha * apply_map(scaling * image, turn)
        along = across + ratio * along

    if paired:
        scaled = scaling * direction
        before = across + ratio * along
        known = inner(scaled, before) + inner(load * direction, direction)
        kept = (scaling * (1.0 + update), residual, scaling, scaling * before + load * direction, direction)
        for i, value in enumerate(kept):
            state[i] = value
        total = with_partner(products(scaling * image), final)
        dense[1 + final] = total
        ends[me] = dense[1 + final, own]
        dots[me] = jnp.broadcast_to(inner(scaled, total), (1, LANES))

        @for_peers
        def _(place, member, target):
            part = pl.ds(pl.multiple_of(place * held, held), held)
            send(dense.at[1 + final, part], ends.at[me], 1 + final, target)
            pltpu.make_async_remote_copy(
                src_ref=dots.at[me], dst_ref=dots.at[me], send_sem=dot_send,
                recv_sem=dot_recv, device_id=target, device_id_type=MESH,
            ).start()

        take(dots.at[rest], dot_recv)
        step_size = norm_now / (known - alpha * jnp.sum(dots[...], axis=0)[:, :1])
        take(ends.at[rest], recv_sem.at[1 + final])
        image = state[3, own] - alpha * (state[2, own] * jnp.sum(ends[...], axis=0))
        out_ref[0] = state[0, own] + state[2, own] * (step_size * state[4, own])
        out_ref[1] = state[1, own] - step_size * image
    else:
        state[0] = scaling * (1.0 + update)
        state[1] = residual
        out_ref[0] = state[0, own]
        out_ref[1] = state[1, own]

    take(others, send_sem.at[0])
    if paired:
        for turn in range(final):
            take(shares.at[turn, rest], send_sem.at[1 + turn])
        for turn in range(1 + final):
            take(mate.at[turn], mate_send.at[turn])
        take(ends.at[rest], send_sem.at[1 + final])
        take(dots.at[rest], dot_send)
    else:
        for slot in range(1, 3 + 2 * ITERS):
            take(blocked.at[0, rest], send_sem.at[slot])


def shards(places, reps, tiles, tile_row, tile_col, scaling):
    count, width, _ = tiles.shape
    halves = width // LANES
    owned = scaling.shape[0] // width
    blocks = owned * places
    assert owned == reps
    turns = 1 + ITERS
    paired = reps % 2 == 0 and places * reps <= 32
    chunk = 16 if blocks % 16 == 0 else blocks
    members = blocks // 2 if paired else blocks
    rows, held = blocks * halves, owned * halves
    hbm = pl.BlockSpec(memory_space=pltpu.HBM)
    vmem = pl.BlockSpec(memory_space=pltpu.VMEM)
    slots = 1 + 2 * turns

    def scratch(*dims):
        return pltpu.VMEM(dims + (LANES,), jnp.float32)

    some, none = (turns, 1) if paired else (1, turns)
    both = pl.pallas_call(
        functools.partial(kernel, (count, blocks, reps, owned, halves, paired)),
        out_shape=pltpu.VMEM((2, held, LANES), jnp.float32),
        in_specs=[hbm] * 4,
        out_specs=vmem,
        scratch_shapes=[
            pltpu.SMEM((count,), jnp.int32),
            pltpu.SMEM((count,), jnp.int32),
            pltpu.VMEM((2 * count, width, width), jnp.float32),
            pltpu.VMEM((chunk, 3 * chunk * halves, width), jnp.bfloat16),
            pltpu.VMEM((blocks, width, LANES), jnp.float32),
            scratch(rows),
            scratch(some + 1, rows),
            scratch(some, rows),
            scratch(some, members if paired else 1, rows),
            scratch(5, rows),
            scratch(members, held),
            scratch(members, 1),
            scratch(none, blocks, halves),
            scratch(none, members, halves),
            scratch(none, blocks, halves),
            pltpu.SemaphoreType.DMA((count,)),
            pltpu.SemaphoreType.DMA,
            pltpu.SemaphoreType.DMA((2,)),
            pltpu.SemaphoreType.DMA((slots,)),
            pltpu.SemaphoreType.DMA((slots,)),
            pltpu.SemaphoreType.DMA((turns,)),
            pltpu.SemaphoreType.DMA((turns,)),
            pltpu.SemaphoreType.DMA,
            pltpu.SemaphoreType.DMA,
        ],
        compiler_params=pltpu.CompilerParams(
            collective_id=0, has_side_effects=True, vmem_limit_bytes=56 * 2**20),
    )(tiles, tile_row, tile_col, scaling.reshape(held, LANES))
    both = both.reshape(2, -1)
    return both[0], both[1]


def solution(mesh):
    placed = (
        P(("groups", "tiles", "rep"), None, None),
        P(("groups", "tiles", "rep")),
        P(("groups", "tiles", "rep")),
        P(("groups", "tiles")),
    )
    return jax.shard_map(
        functools.partial(shards, mesh.shape["tiles"], mesh.shape["rep"]),
        mesh=mesh,
        in_specs=placed,
        out_specs=(P(("groups", "tiles")), P(("groups", "tiles"))),
        check_vma=False,
    )
```

```python
import functools
import jax
import jax.numpy as jnp
from jax import lax
from jax.experimental import pallas as pl
from jax.experimental.pallas import tpu as pltpu
from jax.sharding import PartitionSpec as P

ITERS = 2
LANES = 128
MESH = pl.DeviceIdType.MESH


def split_exact(x):
    high = x.astype(jnp.bfloat16)
    rest = x - high.astype(jnp.float32)
    mid = rest.astype(jnp.bfloat16)
    low = (rest - mid.astype(jnp.float32)).astype(jnp.bfloat16)
    return jnp.concatenate([high, mid, low], axis=0)


def wrap(index, size):
    return jnp.where(index >= size, index - size, index)


def kernel(sizes, tiles_hbm, row_hbm, col_hbm, scaling_ref, out_ref,
           row_ref, col_ref,
           mats, pick, spread, scale_all, dense, mate, shares, state, ends, dots, terms, parcels, blocked,
           tile_sem, scale_sem, index_sem, send_sem, recv_sem, mate_send, mate_recv, dot_send, dot_recv):
    count, blocks, reps, owned, halves, paired = sizes
    places = blocks // owned
    q = lax.axis_index("tiles")
    r = lax.axis_index("rep")
    rows = blocks * halves
    width = halves * LANES
    chunk = pick.shape[0]
    lanes = 2 if paired else 1
    turn_reps = reps // lanes
    mine = r // lanes
    side = r - mine * lanes
    me = q * turn_reps + mine
    members = places * turn_reps
    final = ITERS if paired else -1

    def for_peers(act):
        def column(ahead, first):
            place = wrap(q + ahead, places)
            for turn in reversed(range(first, turn_reps)):
                member = wrap(mine + turn, turn_reps)
                act(place, place * turn_reps + member, {"tiles": place, "rep": member * lanes + side})

        if places <= 8:
            for ahead in range(places - 1, 0, -1):
                column(ahead, 0)
        else:
            pl.loop(1, places)(lambda ahead: column(ahead, 0))
        column(0, 1)

    partner = {"rep": r + 1 - 2 * side}

    def send(source, target_ref, slot, device):
        pltpu.make_async_remote_copy(
            src_ref=source, dst_ref=target_ref, send_sem=send_sem.at[slot],
            recv_sem=recv_sem.at[slot], device_id=device, device_id_type=MESH,
        ).start()

    def take(ref, semaphore):
        pltpu.make_async_copy(ref, ref, semaphore).wait()

    def tile_copy(k):
        return pltpu.make_async_copy(tiles_hbm.at[k], mats.at[count + k], tile_sem.at[k])

    barrier = pltpu.get_barrier_semaphore()

    @for_peers
    def _(place, member, target):
        pl.semaphore_signal(barrier, inc=1, device_id=target, device_id_type=MESH)

    if paired:
        pl.semaphore_signal(barrier, inc=1, device_id=partner, device_id_type=MESH)

    indices = [pltpu.make_async_copy(source, held, index_sem.at[i])
               for i, (source, held) in enumerate(((row_hbm, row_ref), (col_hbm, col_ref)))]
    for copy in indices:
        copy.start()
    for k in range(count):
        tile_copy(k).start()
    held = owned * halves
    own = pl.ds(pl.multiple_of(q * held, held), held)
    own_scale = pltpu.make_async_copy(scaling_ref, scale_all.at[own], scale_sem)
    own_scale.start()

    half_row = lax.broadcasted_iota(jnp.int32, (chunk * halves, width), 0)
    half = lax.broadcasted_iota(jnp.int32, (chunk * halves, width), 1) // LANES

    @pl.loop(0, chunk)
    def _(b):
        hot = jnp.where(half_row == halves * b + half, 1.0, 0.0).astype(jnp.bfloat16)
        pick[b] = jnp.concatenate([hot, hot, hot], axis=0)

    own_scale.wait()
    for copy in indices:
        copy.wait()
    pl.semaphore_wait(barrier, members if paired else members - 1)

    for ahead in range(places - 1, 0, -1):
        pltpu.make_async_remote_copy(
            src_ref=scale_all.at[own], dst_ref=scale_all.at[own],
            send_sem=send_sem.at[0], recv_sem=recv_sem.at[0],
            device_id={"tiles": wrap(q + ahead, places)}, device_id_type=MESH,
        ).start()

    @pl.loop(0, count)
    def _(k):
        tile_copy(k).wait()
        mats[k] = mats[count + k].T

    others = scale_all.at[pl.ds(0, (places - 1) * held)]
    rest = pl.ds(0, members - 1)
    take(others, recv_sem.at[0])

    line = lax.broadcasted_iota(jnp.int32, (rows, LANES), 0)

    def products(vector):
        for first in range(0, blocks, chunk):
            parts = split_exact(vector[first * halves:(first + chunk) * halves]).T

            def widen(b, carry):
                wide = jnp.dot(parts, pick[b], preferred_element_type=jnp.float32)
                for h in range(halves):
                    spread[first + b, h * LANES:(h + 1) * LANES, :] = wide[:, h * LANES:(h + 1) * LANES]
                return carry

            lax.fori_loop(0, chunk, widen, 0, unroll=True)

        def one(matrix, source, place, total):
            x = spread[source].reshape(-1, 8, LANES)
            for h in range(halves):
                block = mats[matrix, :, h * LANES:(h + 1) * LANES].reshape(-1, 8, LANES)
                product = jnp.sum(jnp.sum(block * x, axis=0), axis=0, keepdims=True)
                total = total + jnp.where(line == halves * place + h, product, 0.0)
            return total

        def both(k, total):
            row, col = row_ref[k], col_ref[k]
            total = one(k, col, row, total)
            return one(count + k, row, jnp.where(row == col, -1, col), total)

        return lax.fori_loop(0, count, both, jnp.zeros((rows, LANES), jnp.float32), unroll=8)

    def with_partner(total, turn):
        dense[turn] = total
        pltpu.make_async_remote_copy(
            src_ref=dense.at[turn], dst_ref=mate.at[turn],
            send_sem=mate_send.at[turn], recv_sem=mate_recv.at[turn],
            device_id=partner, device_id_type=MESH).start()
        take(mate.at[turn], mate_recv.at[turn])
        return total + mate[turn]

    def summed_pairs(vector, turn):
        shares[turn, me] = with_partner(products(vector), turn)

        @for_peers
        def _(place, member, target):
            send(shares.at[turn, me], shares.at[turn, me], 1 + turn, target)

        take(shares.at[turn, rest], recv_sem.at[1 + turn])
        return jnp.sum(shares[turn], axis=0)

    def summed_blocks(vector, turn):
        terms[turn] = products(vector).reshape(blocks, halves, LANES)
        parcels[turn, me] = terms[turn, me]
        slot = 1 + 2 * turn

        @for_peers
        def _(place, member, target):
            send(terms.at[turn, member], parcels.at[turn, me], slot, target)

        take(parcels.at[turn, rest], recv_sem.at[slot])
        blocked[turn, me] = jnp.sum(parcels[turn], axis=0)

        @for_peers
        def _(place, member, target):
            send(blocked.at[turn, me], blocked.at[turn, me], slot + 1, target)

        take(blocked.at[turn, rest], recv_sem.at[slot + 1])
        return blocked[turn].reshape(rows, LANES)

    apply_map = summed_pairs if paired else summed_blocks

    def inner(a, b):
        return jnp.sum(a * b, keepdims=True)

    scaling = scale_all[...]
    load = scaling * apply_map(scaling, 0)
    residual = 1.0 - load
    direction = residual
    update = jnp.zeros_like(load)
    norm_now = inner(residual, residual)
    along = apply_map(scaling * direction, 1)
    across = along
    for step in range(ITERS):
        turn = 2 + step
        last = step + 1 == ITERS
        image = scaling * along + load * direction
        alpha = norm_now / inner(direction, image)
        update = update + alpha * direction
        residual = residual - alpha * image
        if last:
            break
        norm_next = inner(residual, residual)
        ratio = norm_next / norm_now
        direction = residual + ratio * direction
        norm_now = norm_next
        if turn == final:
            break
        across = across - alpha * apply_map(scaling * image, turn)
        along = across + ratio * along

    if paired:
        scaled = scaling * direction
        before = across + ratio * along
        known = inner(scaled, before) + inner(load * direction, direction)
        kept = (scaling * (1.0 + update), residual, scaling, scaling * before + load * direction, direction)
        for i, value in enumerate(kept):
            state[i] = value
        total = with_partner(products(scaling * image), final)
        dense[1 + final] = total
        ends[me] = dense[1 + final, own]
        dots[me] = jnp.broadcast_to(inner(scaled, total), (1, LANES))

        @for_peers
        def _(place, member, target):
            part = pl.ds(pl.multiple_of(place * held, held), held)
            send(dense.at[1 + final, part], ends.at[me], 1 + final, target)
            pltpu.make_async_remote_copy(
                src_ref=dots.at[me], dst_ref=dots.at[me], send_sem=dot_send,
                recv_sem=dot_recv, device_id=target, device_id_type=MESH,
            ).start()

        take(dots.at[rest], dot_recv)
        step_size = norm_now / (known - alpha * jnp.sum(dots[...], axis=0)[:, :1])
        take(ends.at[rest], recv_sem.at[1 + final])
        image = state[3, own] - alpha * (state[2, own] * jnp.sum(ends[...], axis=0))
        out_ref[0] = state[0, own] + state[2, own] * (step_size * state[4, own])
        out_ref[1] = state[1, own] - step_size * image
    else:
        state[0] = scaling * (1.0 + update)
        state[1] = residual
        out_ref[0] = state[0, own]
        out_ref[1] = state[1, own]

    take(others, send_sem.at[0])
    if paired:
        for turn in range(final):
            take(shares.at[turn, rest], send_sem.at[1 + turn])
        for turn in range(1 + final):
            take(mate.at[turn], mate_send.at[turn])
        take(ends.at[rest], send_sem.at[1 + final])
        take(dots.at[rest], dot_send)
    else:
        for slot in range(1, 3 + 2 * ITERS):
            take(blocked.at[0, rest], send_sem.at[slot])


def shards(places, reps, tiles, tile_row, tile_col, scaling):
    count, width, _ = tiles.shape
    halves = width // LANES
    owned = scaling.shape[0] // width
    blocks = owned * places
    assert owned == reps
    turns = 1 + ITERS
    paired = reps % 2 == 0 and places * reps <= 32
    chunk = 16 if blocks % 16 == 0 else blocks
    members = blocks // 2 if paired else blocks
    rows, held = blocks * halves, owned * halves
    hbm = pl.BlockSpec(memory_space=pltpu.HBM)
    vmem = pl.BlockSpec(memory_space=pltpu.VMEM)
    slots = 1 + 2 * turns

    def scratch(*dims):
        return pltpu.VMEM(dims + (LANES,), jnp.float32)

    some, none = (turns, 1) if paired else (1, turns)
    both = pl.pallas_call(
        functools.partial(kernel, (count, blocks, reps, owned, halves, paired)),
        out_shape=pltpu.VMEM((2, held, LANES), jnp.float32),
        in_specs=[hbm] * 4,
        out_specs=vmem,
        scratch_shapes=[
            pltpu.SMEM((count,), jnp.int32),
            pltpu.SMEM((count,), jnp.int32),
            pltpu.VMEM((2 * count, width, width), jnp.float32),
            pltpu.VMEM((chunk, 3 * chunk * halves, width), jnp.bfloat16),
            pltpu.VMEM((blocks, width, LANES), jnp.float32),
            scratch(rows),
            scratch(some + 1, rows),
            scratch(some, rows),
            scratch(some, members if paired else 1, rows),
            scratch(5, rows),
            scratch(members, held),
            scratch(members, 1),
            scratch(none, blocks, halves),
            scratch(none, members, halves),
            scratch(none, blocks, halves),
            pltpu.SemaphoreType.DMA((count,)),
            pltpu.SemaphoreType.DMA,
            pltpu.SemaphoreType.DMA((2,)),
            pltpu.SemaphoreType.DMA((slots,)),
            pltpu.SemaphoreType.DMA((slots,)),
            pltpu.SemaphoreType.DMA((turns,)),
            pltpu.SemaphoreType.DMA((turns,)),
            pltpu.SemaphoreType.DMA,
            pltpu.SemaphoreType.DMA,
        ],
        compiler_params=pltpu.CompilerParams(
            collective_id=0, has_side_effects=True, vmem_limit_bytes=56 * 2**20),
    )(tiles, tile_row, tile_col, scaling.reshape(held, LANES))
    both = both.reshape(2, -1)
    return both[0], both[1]


def solution(mesh):
    placed = (
        P(("groups", "tiles", "rep"), None, None),
        P(("groups", "tiles", "rep")),
        P(("groups", "tiles", "rep")),
        P(("groups", "tiles")),
    )
    return jax.shard_map(
        functools.partial(shards, mesh.shape["tiles"], mesh.shape["rep"]),
        mesh=mesh,
        in_specs=placed,
        out_specs=(P(("groups", "tiles")), P(("groups", "tiles"))),
        check_vma=False,
    )
```
